128 devices in a mesh: ctx: 8 (over y, core), uly: 16 (over z, x).
Axes of the slice: x: 4, y: 4, z: 4, core: 2. Of those that a mesh axis runs over, the one named last changes fastest.
Arguments:
- queries: bfloat16 [131072, 2048], P(('ctx', 'uly')), may hold values from -6 to 6
- key_vectors: bfloat16 [131072, 2048], P(('ctx', 'uly')), may hold values from -0.52734375 to 0.52734375
- value_vectors: bfloat16 [131072, 2048], P(('ctx', 'uly')), may hold values from -6 to 6
- level_gates: bfloat16 [131072, 192], P(('ctx', 'uly')), may hold values from 0.049804688 to 1
Outputs:
- attended: bfloat16 [131072, 2048], P(('ctx', 'uly'))
The draws below stay inside these ranges and needn't reach their ends.
All inputs are finite; a program needn't handle non-finite values.
Results may differ from the reference program's by a relative error of at most 0.005.
Values may be sent and summed in bfloat16 or wider, within the bound.
A program may use at most 192 MiB of HBM per device.

```python
import math
import jax
import jax.numpy as jnp
from jax import lax

H = 16
HEAD_DIM = 128
BLOCK = 64
TOKENS = 131072
LEVELS = 12


def shard_levels(rng, dims, shards, least, high):
    gain = 1.0
    for dim, shards_of in shards:
        steps = jax.random.uniform(jax.random.fold_in(jax.random.fold_in(rng, 6), dim), (shards_of,), jnp.float32, least / len(shards), high / len(shards))
        gain = gain * jnp.repeat(jnp.exp(steps), dims[dim] // shards_of).reshape((-1,) + (1,) * (len(dims) - 1 - dim))
    return gain


def centred(own_key, shape, deviation, bound, split=(), kind=jnp.bfloat16):
    values = jax.random.normal(own_key, shape, jnp.float32) * deviation
    if len(split) > 0:
        values = shard_levels(own_key, shape, split, -0.22, 0.18) * values
    return jnp.clip(values, min=-bound, max=bound).astype(kind)


def setup_inputs(seed: int = 0) -> dict:
    streams_of = jax.random.split(jax.random.key(seed), 5)
    queries = centred(streams_of[0], (TOKENS, H * HEAD_DIM), 1.0, 6.0, ((0, 128),))
    key_vectors = centred(streams_of[1], (TOKENS, H * HEAD_DIM), 0.0884, 0.52734375, ((0, 128),))
    value_vectors = centred(streams_of[2], (TOKENS, H * HEAD_DIM), 1.0, 6.0, ((0, 128),))
    level_gates = jnp.clip(jnp.exp(math.log(1.0) - 2.9996462 * jax.random.uniform(streams_of[3], (TOKENS, H * LEVELS), jnp.float32) ** shard_levels(streams_of[3], (TOKENS, H * LEVELS), ((0, 128),), -0.2, 0.2)), 0.049804688, 1.0).astype(jnp.bfloat16)
    return dict(queries=queries, key_vectors=key_vectors, value_vectors=value_vectors, level_gates=level_gates)


def reference(queries, key_vectors, value_vectors, level_gates):
    token_total = queries.shape[0]
    block_total = token_total // BLOCK
    causal = jnp.tril(jnp.ones((BLOCK, BLOCK), dtype=bool))

    def one_head(head_no):
        query_rows = lax.dynamic_slice_in_dim(queries, head_no * HEAD_DIM, HEAD_DIM, 1).astype(jnp.float32)
        key_rows = lax.dynamic_slice_in_dim(key_vectors, head_no * HEAD_DIM, HEAD_DIM, 1).astype(jnp.float32)
        value_rows = lax.dynamic_slice_in_dim(value_vectors, head_no * HEAD_DIM, HEAD_DIM, 1).astype(jnp.float32)
        gate_rows = lax.dynamic_slice_in_dim(level_gates, head_no * LEVELS, LEVELS, 1).astype(jnp.float32)
        query_blocks = query_rows.reshape(block_total, BLOCK, HEAD_DIM)
        key_blocks = key_rows.reshape(block_total, BLOCK, HEAD_DIM)
        value_blocks = value_rows.reshape(block_total, BLOCK, HEAD_DIM)
        scores = jnp.einsum("cid,cjd->cij", query_blocks, key_blocks)
        scores = jnp.where(causal[None], scores, 0.0).astype(jnp.bfloat16)
        scores = lax.optimization_barrier(scores).astype(jnp.float32)
        output = jnp.einsum("cij,cjd->cid", scores, value_blocks).reshape(token_total, HEAD_DIM)
        output = output * (gate_rows[:, 0:1] * (BLOCK ** -0.5))
        current = jnp.einsum("cid,cie->cde", key_blocks, value_blocks)
        for level_no in range(1, LEVELS):
            pair_count = block_total >> level_no
            span_len = BLOCK << (level_no - 1)
            paired = current.reshape(pair_count, 2, HEAD_DIM, HEAD_DIM)
            earlier = lax.optimization_barrier(paired[:, 0].astype(jnp.bfloat16)).astype(jnp.float32)
            later_queries = query_rows.reshape(pair_count, 2, span_len, HEAD_DIM)[:, 1]
            partial_value = jnp.einsum("bte,bef->btf", later_queries, earlier)
            level_weight = gate_rows.reshape(pair_count, 2, span_len, LEVELS)[:, 1, :, level_no]
            level_weight = level_weight * ((BLOCK * 2 ** (level_no - 1)) ** -0.5)
            placed = jnp.zeros((pair_count, 2, span_len, HEAD_DIM), jnp.float32)
            placed = placed.at[:, 1].set(partial_value * level_weight[..., None])
            output = output + placed.reshape(token_total, HEAD_DIM)
            current = paired[:, 0] + paired[:, 1]
        return output

    stacked = lax.map(one_head, jnp.arange(H, dtype=jnp.int32))
    return jnp.transpose(stacked, (1, 0, 2)).reshape(token_total, H * HEAD_DIM).astype(jnp.bfloat16)
```

```python
import functools
import jax
import jax.numpy as jnp
from jax import lax
from jax.experimental import pallas as pl
from jax.experimental.pallas import tpu as pltpu
from jax.sharding import PartitionSpec as P

D = 128
BLOCK = 64
TILE = 256
LEVELS = 12
FIRST_REMOTE = 5
STEPS = 7
HC = 2
LAG = 3
F32 = jnp.float32
BF16 = jnp.bfloat16
MESH = pl.DeviceIdType.MESH


def dot_nt(a, b):
    return lax.dot_general(a, b, (((1,), (1,)), ((), ())), preferred_element_type=F32)


def dot_nn(a, b):
    return lax.dot_general(a, b, (((1,), (0,)), ((), ())), preferred_element_type=F32)


def kernel(
    heads,
    q_hbm, k_hbm, v_hbm, g_hbm, o_hbm,
    q_s, k_s, v_s, g_s, vt_s, gate_s, acc_s, cur_s, near_s, send_s, recv_s, out_s,
    in_sem, gate_sem, out_sem, send_sem, recv_sem,
):
    rows = q_s.shape[0]
    tiles = rows // TILE
    chunks = heads // HC
    wide = HC * D

    ctx = lax.axis_index("ctx")
    uly = lax.axis_index("uly")
    core, y = ctx % 2, ctx // 2
    x, z = uly % 4, uly // 4
    x_flip = x + 1 - 2 * (x % 2)
    z_flip = z + 1 - 2 * (z % 2)
    y_flip = y + 1 - 2 * (y % 2)
    partners = (
        (ctx, z * 4 + x_flip),
        (ctx, z * 4 + 3 - x),
        (ctx, z_flip * 4 + x),
        (ctx, (3 - z) * 4 + x),
        (y * 2 + 1 - core, uly),
        (y_flip * 2 + core, uly),
        ((3 - y) * 2 + core, uly),
    )
    bits = (x % 2, x // 2, z % 2, z // 2, core, y % 2, y // 2)

    def columns(c):
        return pl.ds(pl.multiple_of(c * wide, wide), wide)

    def load(which, c):
        hbm, vmem = ((k_hbm, k_s), (v_hbm, v_s), (q_hbm, q_s))[which]
        return pltpu.make_async_copy(
            hbm.at[:, columns(c)], vmem.at[:, columns(c)], in_sem.at[which, c]
        )

    def store(h):
        cols = pl.ds(pl.multiple_of(h * D, D), D)
        return pltpu.make_async_copy(out_s.at[:, cols], o_hbm.at[:, cols], out_sem.at[h])

    def message(step, c):
        part = pl.ds(c * HC, HC)
        return pltpu.make_async_remote_copy(
            src_ref=send_s.at[step, part],
            dst_ref=recv_s.at[step, part],
            send_sem=send_sem.at[step, c],
            recv_sem=recv_sem.at[step, c],
            device_id=partners[step],
            device_id_type=MESH,
        )

    gate_load = pltpu.make_async_copy(g_hbm, g_s, gate_sem)
    gate_load.start()

    @pl.loop(0, chunks)
    def _(c):
        load(0, c).start()
        load(1, c).start()

    @pl.loop(0, chunks)
    def _(c):
        load(2, c).start()

    barrier = pltpu.get_barrier_semaphore()
    for partner in partners:
        pl.semaphore_signal(barrier, inc=1, device_id=partner, device_id_type=MESH)

    gate_load.wait()
    row = lax.broadcasted_iota(jnp.int32, (heads * 16, heads * LEVELS), 0)
    col = lax.broadcasted_iota(jnp.int32, (heads * 16, heads * LEVELS), 1)
    pick = (col == (row // 16) * LEVELS + row % 16) & (row % 16 < LEVELS)
    table = dot_nt(jnp.where(pick, 1.0, 0.0).astype(BF16), g_s[...])
    level = lax.broadcasted_iota(jnp.int32, (heads * 16, 1), 0) % 16
    scale = jnp.zeros((heads * 16, 1), F32)
    for l in range(LEVELS):
        factor = jnp.float32((BLOCK * 2 ** max(l - 1, 0)) ** -0.5)
        if l >= FIRST_REMOTE:
            factor = factor * bits[l - FIRST_REMOTE].astype(F32)
        scale = jnp.where(level == l, factor, scale)
    gate_s[...] = (table * scale).reshape(heads, 16, rows)

    pl.semaphore_wait(barrier, STEPS)

    def states(c):
        load(0, c).wait()
        load(1, c).wait()
        for part in range(HC):
            h = c * HC + part
            cols = pl.ds(pl.multiple_of(h * D, D), D)
            vt = v_s[:, cols].T
            vt_s[h] = vt
            sums = [
                dot_nn(vt[:, i * TILE:(i + 1) * TILE], k_s[i * TILE:(i + 1) * TILE, cols])
                for i in range(tiles)
            ]
            first = sums[0] + sums[1]
            near_s[h, 0] = sums[0].astype(BF16)
            near_s[h, 1] = sums[2].astype(BF16)
            near_s[h, 2] = first.astype(BF16)
            total = first + (sums[2] + sums[3])
            cur_s[h] = total
            send_s[0, h] = total.astype(BF16)
        message(0, c).start()

    def exchange(step, c):
        message(step, c).wait_recv()
        if step + 1 < STEPS:
            for part in range(HC):
                h = c * HC + part
                total = cur_s[h] + recv_s[step, h].astype(F32)
                cur_s[h] = total
                send_s[step + 1, h] = total.astype(BF16)
            message(step + 1, c).start()

    def exchanges(slot):
        for step in reversed(range(STEPS)):
            c = slot - LAG * (step + 1)

            @pl.when((c >= 0) & (c < chunks))
            def _():
                exchange(step, c)

    half = TILE // 2
    s_at = lax.broadcasted_iota(jnp.int32, (half, half), 0)
    t_at = lax.broadcasted_iota(jnp.int32, (half, half), 1)
    own = (s_at // BLOCK == t_at // BLOCK) & (s_at <= t_at)
    before = s_at // BLOCK < t_at // BLOCK

    def local(h):
        cols = pl.ds(pl.multiple_of(h * D, D), D)
        for i in range(tiles):
            span = slice(i * TILE, (i + 1) * TILE)
            q_tile = q_s[span, cols]
            scores = dot_nt(k_s[span, cols], q_tile)
            gate = [gate_s[h, l:l + 1, span] for l in range(FIRST_REMOTE)]

            def weigh(at):
                part = slice(at, at + half)
                return jnp.where(own, gate[0][:, part], jnp.where(before, gate[1][:, part], 0.0))

            top = jnp.concatenate(
                [scores[:half, :half] * weigh(0), scores[:half, half:] * gate[2][:, half:]], axis=1
            )
            low = jnp.concatenate(
                [jnp.zeros((half, half), F32), scores[half:, half:] * weigh(half)], axis=1
            )
            weights = jnp.concatenate([top.astype(BF16), low.astype(BF16)], axis=0)
            out = dot_nn(vt_s[h, :, span], weights)
            if i % 2 == 1:
                out = out + dot_nt(near_s[h, i // 2], q_tile) * gate[3]
            if i >= 2:
                out = out + dot_nt(near_s[h, 2], q_tile) * gate[4]
            acc_s[h, :, span] = out

    def remote(h):
        cols = pl.ds(pl.multiple_of(h * D, D), D)
        for i in range(tiles):
            span = slice(i * TILE, (i + 1) * TILE)
            q_tile = q_s[span, cols]
            out = acc_s[h, :, span]
            for step in range(STEPS):
                l = FIRST_REMOTE + step
                out = out + dot_nt(recv_s[step, h], q_tile) * gate_s[h, l:l + 1, span]
            out_s[span, cols] = out.T.astype(BF16)
        store(h).start()

    @pl.loop(0, chunks)
    def _(c):
        states(c)
        exchanges(c)

    @pl.loop(0, chunks)
    def _(c):
        load(2, c).wait()

    @pl.loop(0, heads)
    def _(h):
        local(h)
        exchanges(chunks + h)

    @pl.loop(0, heads)
    def _(h):
        exchanges(chunks + heads + h)
        remote(h)

    @pl.loop(0, heads)
    def _(h):
        store(h).wait()

    for step in range(STEPS):
        @pl.loop(0, chunks)
        def _(c):
            message(step, c).wait_send()


def shards(queries, key_vectors, value_vectors, level_gates):
    rows, width = queries.shape
    heads = width // D
    chunks = heads // HC
    hbm = pl.BlockSpec(memory_space=pl.ANY)
    return pl.pallas_call(
        functools.partial(kernel, heads),
        out_shape=jax.ShapeDtypeStruct((rows, width), BF16),
        in_specs=[hbm] * 4,
        out_specs=hbm,
        scratch_shapes=[
            pltpu.VMEM((rows, width), BF16),
            pltpu.VMEM((rows, width), BF16),
            pltpu.VMEM((rows, width), BF16),
            pltpu.VMEM((rows, heads * LEVELS), BF16),
            pltpu.VMEM((heads, D, rows), BF16),
            pltpu.VMEM((heads, 16, rows), F32),
            pltpu.VMEM((heads, D, rows), F32),
            pltpu.VMEM((heads, D, D), F32),
            pltpu.VMEM((heads, 3, D, D), BF16),
            pltpu.VMEM((STEPS, heads, D, D), BF16),
            pltpu.VMEM((STEPS, heads, D, D), BF16),
            pltpu.VMEM((rows, width), BF16),
            pltpu.SemaphoreType.DMA((3, chunks)),
            pltpu.SemaphoreType.DMA,
            pltpu.SemaphoreType.DMA((heads,)),
            pltpu.SemaphoreType.DMA((STEPS, chunks)),
            pltpu.SemaphoreType.DMA((STEPS, chunks)),
        ],
        compiler_params=pltpu.CompilerParams(
            collective_id=0, has_side_effects=True, vmem_limit_bytes=56 * 1024 * 1024
        ),
        name="fenwick",
    )(queries, key_vectors, value_vectors, level_gates)


def solution(mesh):
    spec = P(("ctx", "uly"), None)
    return jax.shard_map(
        shards, mesh=mesh, in_specs=(spec,) * 4, out_specs=spec, check_vma=False
    )
```

```python
import functools
import jax
import jax.numpy as jnp
from jax import lax
from jax.experimental import pallas as pl
from jax.experimental.pallas import tpu as pltpu
from jax.sharding import PartitionSpec as P

D = 128
BLOCK = 64
TILE = 256
LEVELS = 12
FIRST_REMOTE = 5
STEPS = 7
HC = 2
VL = 58
OFF = (3, 6, 9, 12, 15, 18, 21)
LP = 2
F32 = jnp.float32
BF16 = jnp.bfloat16
MESH = pl.DeviceIdType.MESH


def dot_nt(a, b):
    return lax.dot_general(a, b, (((1,), (1,)), ((), ())), preferred_element_type=F32)


def dot_nn(a, b):
    return lax.dot_general(a, b, (((1,), (0,)), ((), ())), preferred_element_type=F32)


def kernel(
    heads,
    q_hbm, k_hbm, v_hbm, g_hbm, o_ref,
    q_s, k_s, v_s, g_s, gate_s, acc_s, cur_s, near_s, send_s, recv_s,
    in_sem, gate_sem, send_sem, recv_sem,
):
    rows = q_s.shape[0]
    tiles = rows // TILE
    chunks = heads // HC
    wide = HC * D

    ctx = lax.axis_index("ctx")
    uly = lax.axis_index("uly")
    core, y = ctx % 2, ctx // 2
    x, z = uly % 4, uly // 4
    x_flip = x + 1 - 2 * (x % 2)
    z_flip = z + 1 - 2 * (z % 2)
    y_flip = y + 1 - 2 * (y % 2)
    partners = (
        (ctx, z * 4 + x_flip),
        (ctx, z * 4 + 3 - x),
        (ctx, z_flip * 4 + x),
        (ctx, (3 - z) * 4 + x),
        (y * 2 + 1 - core, uly),
        (y_flip * 2 + core, uly),
        ((3 - y) * 2 + core, uly),
    )
    bits = (x % 2, x // 2, z % 2, z // 2, core, y % 2, y // 2)

    def columns(c):
        return pl.ds(pl.multiple_of(c * wide, wide), wide)

    def load(which, c):
        hbm, vmem = ((k_hbm, k_s), (v_hbm, v_s), (q_hbm, q_s))[which]
        return pltpu.make_async_copy(
            hbm.at[:, columns(c)], vmem.at[:, columns(c)], in_sem.at[which, c]
        )

    def message(step, c):
        return pltpu.make_async_remote_copy(
            src_ref=send_s.at[step, c],
            dst_ref=recv_s.at[step, c],
            send_sem=send_sem.at[step, c],
            recv_sem=recv_sem.at[step, c],
            device_id=partners[step],
            device_id_type=MESH,
        )

    gate_load = pltpu.make_async_copy(g_hbm, g_s, gate_sem)
    gate_load.start()

    @pl.loop(0, chunks)
    def _(c):
        load(0, c).start()
        load(1, c).start()

    @pl.loop(0, chunks)
    def _(c):
        load(2, c).start()

    barrier = pltpu.get_barrier_semaphore()
    for partner in partners:
        pl.semaphore_signal(barrier, inc=1, device_id=partner, device_id_type=MESH)

    pl.semaphore_wait(barrier, STEPS)

    def states(c):
        load(0, c).wait()
        load(1, c).wait()
        for part in range(HC):
            h = c * HC + part
            cols = pl.ds(pl.multiple_of(h * D, D), D)
            vt = v_s[:, cols].T
            sums = [
                dot_nn(vt[:, i * TILE:(i + 1) * TILE], k_s[i * TILE:(i + 1) * TILE, cols])
                for i in range(tiles)
            ]
            first = sums[0] + sums[1]
            near_s[h, 0] = sums[0].astype(BF16)
            near_s[h, 1] = sums[2].astype(BF16)
            near_s[h, 2] = first.astype(BF16)
            total = first + (sums[2] + sums[3])
            cur_s[h] = total
            send_s[0, c, part * D:(part + 1) * D] = total.astype(BF16)
        message(0, c).start()

    def exchange(step, c):
        message(step, c).wait_recv()
        if step + 1 < STEPS:
            for part in range(HC):
                h = c * HC + part
                total = cur_s[h] + recv_s[step, c, part * D:(part + 1) * D].astype(F32)
                cur_s[h] = total
                send_s[step + 1, c, part * D:(part + 1) * D] = total.astype(BF16)
            message(step + 1, c).start()

    def exchanges(slot):
        for step in reversed(range(STEPS)):
            c = slot - OFF[step]

            @pl.when((c >= 0) & (c < chunks))
            def _():
                exchange(step, c)

    half = TILE // 2
    s_at = lax.broadcasted_iota(jnp.int32, (half, half), 0)
    t_at = lax.broadcasted_iota(jnp.int32, (half, half), 1)
    own = (s_at // BLOCK == t_at // BLOCK) & (s_at <= t_at)
    before = s_at // BLOCK < t_at // BLOCK

    def local(h):
        cols = pl.ds(pl.multiple_of(h * D, D), D)
        for i in range(tiles):
            span = slice(i * TILE, (i + 1) * TILE)
            q_tile = q_s[span, cols]
            scores = dot_nt(k_s[span, cols], q_tile)
            gate = [gate_s[h, l:l + 1, span] for l in range(3)]

            def weigh(at):
                part = slice(at, at + half)
                return jnp.where(own, gate[0][:, part], jnp.where(before, gate[1][:, part], 0.0))

            top = jnp.concatenate(
                [scores[:half, :half] * weigh(0), scores[:half, half:] * gate[2][:, half:]], axis=1
            )
            low = jnp.concatenate(
                [jnp.zeros((half, half), F32), scores[half:, half:] * weigh(half)], axis=1
            )
            weights = jnp.concatenate([top.astype(BF16), low.astype(BF16)], axis=0)
            acc_s[h, span] = dot_nn(weights.T, v_s[span, cols])

    def remote(c, part):
        h = c * HC + part
        cols = pl.ds(pl.multiple_of(h * D, D), D)
        for i in range(tiles):
            span = slice(i * TILE, (i + 1) * TILE)
            q_tile = q_s[span, cols]
            parts = [(FIRST_REMOTE + st, recv_s[st, c, part * D:(part + 1) * D]) for st in range(STEPS)]
            if i % 2 == 1:
                parts.append((3, near_s[h, i // 2]))
            if i >= 2:
                parts.append((4, near_s[h, 2]))
            reads = dot_nt(jnp.concatenate([state for _, state in parts], axis=0), q_tile)
            total = jnp.zeros((D, TILE), F32)
            for at, (l, _) in enumerate(parts):
                total = total + reads[at * D:(at + 1) * D] * gate_s[h, l:l + 1, span]
            o_ref[span, cols] = (total.T + acc_s[h, span]).astype(BF16)

    @pl.loop(0, chunks)
    def _(c):
        exchanges(c)
        states(c)

    gate_load.wait()
    row = lax.broadcasted_iota(jnp.int32, (heads * 16, heads * LEVELS), 0)
    col = lax.broadcasted_iota(jnp.int32, (heads * 16, heads * LEVELS), 1)
    pick = (col == (row // 16) * LEVELS + row % 16) & (row % 16 < LEVELS)
    table = dot_nn(jnp.where(pick, 1.0, 0.0).astype(BF16), g_s[...])
    level = lax.broadcasted_iota(jnp.int32, (heads * 16, 1), 0) % 16
    scale = jnp.zeros((heads * 16, 1), F32)
    for l in range(LEVELS):
        factor = jnp.float32((BLOCK * 2 ** max(l - 1, 0)) ** -0.5)
        if l >= FIRST_REMOTE:
            factor = factor * bits[l - FIRST_REMOTE].astype(F32)
        scale = jnp.where(level == l, factor, scale)
    gate_s[...] = (table * scale).reshape(heads, 16, rows)

    @pl.loop(0, chunks)
    def _(c):
        load(2, c).wait()

    @pl.loop(0, heads // LP)
    def _(n):
        exchanges(chunks + n)
        for part in range(LP):
            local(n * LP + part)

    done = chunks + heads // LP
    idle = max(0, OFF[-1] - done)

    @pl.loop(0, idle)
    def _(n):
        exchanges(done + n)

    @pl.loop(0, chunks)
    def _(c):
        exchanges(done + idle + c)
        for part in range(HC):
            remote(c, part)

    for step in range(STEPS):
        @pl.loop(0, chunks)
        def _(c):
            message(step, c).wait_send()


def shards(queries, key_vectors, value_vectors, level_gates):
    rows, width = queries.shape
    heads = width // D
    chunks = heads // HC
    hbm = pl.BlockSpec(memory_space=pltpu.HBM)
    return pl.pallas_call(
        functools.partial(kernel, heads),
        out_shape=pltpu.VMEM((rows, width), BF16),
        in_specs=[hbm] * 4,
        out_specs=pl.BlockSpec(memory_space=pltpu.VMEM),
        scratch_shapes=[
            pltpu.VMEM((rows, width), BF16),
            pltpu.VMEM((rows, width), BF16),
            pltpu.VMEM((rows, width), BF16),
            pltpu.VMEM((heads * LEVELS, rows), BF16),
                        pltpu.VMEM((heads, 16, rows), F32),
            pltpu.VMEM((heads, rows, D), F32),
            pltpu.VMEM((heads, D, D), F32),
            pltpu.VMEM((heads, 3, D, D), BF16),
            pltpu.VMEM((STEPS, chunks, HC * D, D), BF16),
            pltpu.VMEM((STEPS, chunks, HC * D, D), BF16),
            pltpu.SemaphoreType.DMA((3, chunks)),
            pltpu.SemaphoreType.DMA,
            pltpu.SemaphoreType.DMA((STEPS, chunks)),
            pltpu.SemaphoreType.DMA((STEPS, chunks)),
        ],
        compiler_params=pltpu.CompilerParams(
            collective_id=0, has_side_effects=True, vmem_limit_bytes=VL * 1024 * 1024
        ),
        name="fenwick",
    )(queries, key_vectors, value_vectors, level_gates.T)


def solution(mesh):
    spec = P(("ctx", "uly"), None)
    return jax.shard_map(
        shards, mesh=mesh, in_specs=(spec,) * 4, out_specs=spec, check_vma=False
    )
```

```python
import functools
import jax
import jax.numpy as jnp
from jax import lax
from jax.experimental import pallas as pl
from jax.experimental.pallas import tpu as pltpu
from jax.sharding import PartitionSpec as P

D = 128
BLOCK = 64
TILE = 256
LEVELS = 12
FIRST_REMOTE = 5
STEPS = 7
UNIFORM = 5
HC = 2
GS = 2
VL = 58
OFF = (4, 7, 10, 13, 14, 16, 17)
LP = 2
F32 = jnp.float32
BF16 = jnp.bfloat16
MESH = pl.DeviceIdType.MESH


def dot_nt(a, b):
    return lax.dot_general(a, b, (((1,), (1,)), ((), ())), preferred_element_type=F32)


def dot_nn(a, b):
    return lax.dot_general(a, b, (((1,), (0,)), ((), ())), preferred_element_type=F32)


def kernel(
    heads,
    q_hbm, k_hbm, v_hbm, g_hbm, o_ref,
    q_s, k_s, v_s, g_s, gate_s, acc_s, cur_s, near_s, send_s, recv_s, pair_s, side_s,
    in_sem, gate_sem, send_sem, recv_sem,
):
    rows = q_s.shape[0]
    tiles = rows // TILE
    chunks = heads // HC
    wide = HC * D

    ctx = lax.axis_index("ctx")
    uly = lax.axis_index("uly")
    core, y = ctx % 2, ctx // 2
    x, z = uly % 4, uly // 4
    x_flip = x + 1 - 2 * (x % 2)
    z_flip = z + 1 - 2 * (z % 2)
    y_flip = y + 1 - 2 * (y % 2)
    y_far = y + 2 - 4 * (y // 2)
    partners = (
        (ctx, z * 4 + x_flip),
        (ctx, z * 4 + 3 - x),
        (ctx, z_flip * 4 + x),
        (ctx, (3 - z) * 4 + x),
        (y * 2 + 1 - core, uly),
        (y_flip * 2 + core, uly),
        ((3 - y) * 2 + core, uly),
        (y_far * 2 + core, uly),
    )
    bits = (x % 2, x // 2, z % 2, z // 2, core, y % 2, y // 2)

    sends = (y % 2 == 0, y < 2, y < 2)

    def columns(c):
        return pl.ds(pl.multiple_of(c * wide, wide), wide)

    def load(which, c):
        hbm, vmem = ((k_hbm, k_s), (v_hbm, v_s), (q_hbm, q_s))[which]
        return pltpu.make_async_copy(
            hbm.at[:, columns(c)], vmem.at[:, columns(c)], in_sem.at[which, c]
        )

    def message(step, c):
        return pltpu.make_async_remote_copy(
            src_ref=send_s.at[step, c],
            dst_ref=recv_s.at[step, c],
            send_sem=send_sem.at[step, c],
            recv_sem=recv_sem.at[step, c],
            device_id=partners[step],
            device_id_type=MESH,
        )

    def column(k, c):
        span = pl.ds(0, HC * D)
        return pltpu.make_async_remote_copy(
            src_ref=send_s.at[UNIFORM, c],
            dst_ref=pair_s.at[c, span] if k == 0 else side_s.at[k - 1, c],
            send_sem=send_sem.at[UNIFORM + k, c],
            recv_sem=recv_sem.at[UNIFORM + k, c],
            device_id=partners[UNIFORM + k],
            device_id_type=MESH,
        )

    def forward(c):
        return pltpu.make_async_remote_copy(
            src_ref=pair_s.at[c],
            dst_ref=pair_s.at[c],
            send_sem=send_sem.at[UNIFORM + 3, c],
            recv_sem=recv_sem.at[UNIFORM + 3, c],
            device_id=partners[UNIFORM - 1],
            device_id_type=MESH,
        )

    gate_load = pltpu.make_async_copy(g_hbm, g_s, gate_sem)
    gate_load.start()

    @pl.loop(0, chunks)
    def _(c):
        load(0, c).start()
        load(1, c).start()

    @pl.loop(0, chunks)
    def _(c):
        load(2, c).start()

    pair_s[...] = jnp.zeros_like(pair_s)
    barrier = pltpu.get_barrier_semaphore()
    for partner in partners:
        pl.semaphore_signal(barrier, inc=1, device_id=partner, device_id_type=MESH)

    pl.semaphore_wait(barrier, len(partners))

    def states(c):
        load(0, c).wait()
        load(1, c).wait()
        for part in range(HC):
            h = c * HC + part
            cols = pl.ds(pl.multiple_of(h * D, D), D)
            vt = v_s[:, cols].T
            sums = [
                dot_nn(vt[:, i * TILE:(i + 1) * TILE], k_s[i * TILE:(i + 1) * TILE, cols])
                for i in range(tiles)
            ]
            first = sums[0] + sums[1]
            near_s[h, 0] = sums[0].astype(BF16)
            near_s[h, 1] = sums[2].astype(BF16)
            near_s[h, 2] = first.astype(BF16)
            total = first + (sums[2] + sums[3])
            cur_s[h] = total
            send_s[0, c, part * D:(part + 1) * D] = total.astype(BF16)
        message(0, c).start()

    def advance(step, c):
        for part in range(HC):
            h = c * HC + part
            rows_of = slice(part * D, (part + 1) * D)
            total = cur_s[h] + recv_s[step, c, rows_of].astype(F32)
            cur_s[h] = total
            send_s[step + 1, c, rows_of] = total.astype(BF16)

    def exchange(step, c):
        owner = core == c % 2
        if step < UNIFORM:
            message(step, c).wait_recv()
        if step + 1 < UNIFORM:
            advance(step, c)
            message(step + 1, c).start()
        elif step + 1 == UNIFORM:

            @pl.when(owner)
            def _():
                advance(step, c)
                for k in range(3):
                    pl.when(sends[k])(column(k, c).start)

        elif step == UNIFORM:

            @pl.when(owner)
            def _():
                pl.when(y % 2 == 1)(column(0, c).wait_recv)

                @pl.when(y >= 2)
                def _():
                    column(1, c).wait_recv()
                    column(2, c).wait_recv()
                    pair_s[c, HC * D:] = (
                        side_s[0, c].astype(F32) + side_s[1, c].astype(F32)
                    ).astype(BF16)

                forward(c).start()

        else:

            @pl.when(core != c % 2)
            def _():
                forward(c).wait_recv()

    def exchanges(slot):
        for step in reversed(range(STEPS)):
            c = slot - OFF[step]

            @pl.when((c >= 0) & (c < chunks))
            def _():
                exchange(step, c)

    def gates():
        gate_load.wait()
        row = lax.broadcasted_iota(jnp.int32, (heads * 16, heads * LEVELS), 0)
        col = lax.broadcasted_iota(jnp.int32, (heads * 16, heads * LEVELS), 1)
        pick = (col == (row // 16) * LEVELS + row % 16) & (row % 16 < LEVELS)
        table = dot_nn(jnp.where(pick, 1.0, 0.0).astype(BF16), g_s[...])
        level = lax.broadcasted_iota(jnp.int32, (heads * 16, 1), 0) % 16
        scale = jnp.zeros((heads * 16, 1), F32)
        for l in range(LEVELS):
            factor = jnp.float32((BLOCK * 2 ** max(l - 1, 0)) ** -0.5)
            if l >= FIRST_REMOTE:
                factor = factor * bits[l - FIRST_REMOTE].astype(F32)
            scale = jnp.where(level == l, factor, scale)
        gate_s[...] = (table * scale).reshape(heads, 16, rows)

    half = TILE // 2
    s_at = lax.broadcasted_iota(jnp.int32, (half, half), 0)
    t_at = lax.broadcasted_iota(jnp.int32, (half, half), 1)
    own = (s_at // BLOCK == t_at // BLOCK) & (s_at <= t_at)
    before = s_at // BLOCK < t_at // BLOCK

    def local(h):
        cols = pl.ds(pl.multiple_of(h * D, D), D)
        for i in range(tiles):
            span = slice(i * TILE, (i + 1) * TILE)
            q_tile = q_s[span, cols]
            scores = dot_nt(k_s[span, cols], q_tile)
            gate = [gate_s[h, l:l + 1, span] for l in range(3)]

            def weigh(at):
                part = slice(at, at + half)
                return jnp.where(own, gate[0][:, part], jnp.where(before, gate[1][:, part], 0.0))

            top = jnp.concatenate(
                [scores[:half, :half] * weigh(0), scores[:half, half:] * gate[2][:, half:]], axis=1
            )
            low = jnp.concatenate(
                [jnp.zeros((half, half), F32), scores[half:, half:] * weigh(half)], axis=1
            )
            weights = jnp.concatenate([top.astype(BF16), low.astype(BF16)], axis=0)
            acc_s[h, span] = dot_nn(weights.T, v_s[span, cols])

    def remote(c, part):
        h = c * HC + part
        cols = pl.ds(pl.multiple_of(h * D, D), D)
        for i in range(tiles):
            span = slice(i * TILE, (i + 1) * TILE)
            q_tile = q_s[span, cols]
            parts = [(FIRST_REMOTE + st, recv_s[st, c, part * D:(part + 1) * D]) for st in range(UNIFORM)]
            for st in range(UNIFORM, STEPS):
                at = (st - UNIFORM) * HC * D + part * D
                parts.append((FIRST_REMOTE + st, pair_s[c, at:at + D]))
            if i % 2 == 1:
                parts.append((3, near_s[h, i // 2]))
            if i >= 2:
                parts.append((4, near_s[h, 2]))
            reads = dot_nt(jnp.concatenate([state for _, state in parts], axis=0), q_tile)
            total = jnp.zeros((D, TILE), F32)
            for at, (l, _) in enumerate(parts):
                total = total + reads[at * D:(at + 1) * D] * gate_s[h, l:l + 1, span]
            o_ref[span, cols] = (total.T + acc_s[h, span]).astype(BF16)

    @pl.loop(0, chunks)
    def _(c):
        exchanges(c)
        states(c)

        @pl.when(c == GS)
        def _():
            gates()

    @pl.loop(0, chunks)
    def _(c):
        load(2, c).wait()

    @pl.loop(0, heads // LP)
    def _(n):
        exchanges(chunks + n)
        for part in range(LP):
            local(n * LP + part)

    done = chunks + heads // LP
    idle = max(0, OFF[-1] - done)

    @pl.loop(0, idle)
    def _(n):
        exchanges(done + n)

    @pl.loop(0, chunks)
    def _(c):
        exchanges(done + idle + c)
        for part in range(HC):
            remote(c, part)

    @pl.loop(0, chunks)
    def _(c):
        for step in range(UNIFORM):
            message(step, c).wait_send()

        @pl.when(core == c % 2)
        def _():
            for k in range(3):
                pl.when(sends[k])(column(k, c).wait_send)
            forward(c).wait_send()


def shards(queries, key_vectors, value_vectors, level_gates):
    rows, width = queries.shape
    heads = width // D
    chunks = heads // HC
    hbm = pl.BlockSpec(memory_space=pltpu.HBM)
    return pl.pallas_call(
        functools.partial(kernel, heads),
        out_shape=pltpu.VMEM((rows, width), BF16),
        in_specs=[hbm] * 4,
        out_specs=pl.BlockSpec(memory_space=pltpu.VMEM),
        scratch_shapes=[
            pltpu.VMEM((rows, width), BF16),
            pltpu.VMEM((rows, width), BF16),
            pltpu.VMEM((rows, width), BF16),
            pltpu.VMEM((heads * LEVELS, rows), BF16),
            pltpu.VMEM((heads, 16, rows), F32),
            pltpu.VMEM((heads, rows, D), F32),
            pltpu.VMEM((heads, D, D), F32),
            pltpu.VMEM((heads, 3, D, D), BF16),
            pltpu.VMEM((UNIFORM + 1, chunks, HC * D, D), BF16),
            pltpu.VMEM((UNIFORM, chunks, HC * D, D), BF16),
            pltpu.VMEM((chunks, 2 * HC * D, D), BF16),
            pltpu.VMEM((2, chunks, HC * D, D), BF16),
            pltpu.SemaphoreType.DMA((3, chunks)),
            pltpu.SemaphoreType.DMA,
            pltpu.SemaphoreType.DMA((UNIFORM + 4, chunks)),
            pltpu.SemaphoreType.DMA((UNIFORM + 4, chunks)),
        ],
        compiler_params=pltpu.CompilerParams(
            collective_id=0, has_side_effects=True, vmem_limit_bytes=VL * 1024 * 1024
        ),
        name="fenwick",
    )(queries, key_vectors, value_vectors, level_gates.T)


def solution(mesh):
    spec = P(("ctx", "uly"), None)
    return jax.shard_map(
        shards, mesh=mesh, in_specs=(spec,) * 4, out_specs=spec, check_vma=False
    )
```

```python
import functools
import jax
import jax.numpy as jnp
from jax import lax
from jax.experimental import pallas as pl
from jax.experimental.pallas import tpu as pltpu
from jax.sharding import PartitionSpec as P

D = 128
BLOCK = 64
TILE = 256
LEVELS = 12
FIRST_REMOTE = 5
STEPS = 7
UNIFORM = 5
HC = 2
GS = 2
VL = 58
OFF = (4, 7, 10, 13, 14, 16, 17)
LP = 2
F32 = jnp.float32
BF16 = jnp.bfloat16
MESH = pl.DeviceIdType.MESH


def dot_nt(a, b):
    return lax.dot_general(a, b, (((1,), (1,)), ((), ())), preferred_element_type=F32)


def dot_nn(a, b):
    return lax.dot_general(a, b, (((1,), (0,)), ((), ())), preferred_element_type=F32)


def kernel(
    heads,
    q_hbm, k_hbm, v_hbm, g_hbm, o_ref,
    q_s, k_s, v_s, g_s, gate_s, acc_s, cur_s, near_s, send_s, recv_s, pair_s, side_s,
    in_sem, gate_sem, send_sem, recv_sem,
):
    rows = q_s.shape[0]
    tiles = rows // TILE
    chunks = heads // HC
    wide = HC * D

    ctx = lax.axis_index("ctx")
    uly = lax.axis_index("uly")
    core, y = ctx % 2, ctx // 2
    x, z = uly % 4, uly // 4
    x_flip = x + 1 - 2 * (x % 2)
    z_flip = z + 1 - 2 * (z % 2)
    y_flip = y + 1 - 2 * (y % 2)
    y_far = y + 2 - 4 * (y // 2)
    partners = (
        (ctx, z * 4 + x_flip),
        (ctx, z * 4 + 3 - x),
        (ctx, z_flip * 4 + x),
        (ctx, (3 - z) * 4 + x),
        (y * 2 + 1 - core, uly),
        (y_flip * 2 + core, uly),
        ((3 - y) * 2 + core, uly),
        (y_far * 2 + core, uly),
    )
    bits = (x % 2, x // 2, z % 2, z // 2, core, y % 2, y // 2)

    sends = (y % 2 == 0, y < 2, y < 2)

    def columns(c):
        return pl.ds(pl.multiple_of(c * wide, wide), wide)

    def load(which, c):
        hbm, vmem = ((k_hbm, k_s), (v_hbm, v_s), (q_hbm, q_s))[which]
        return pltpu.make_async_copy(
            hbm.at[:, columns(c)], vmem.at[:, columns(c)], in_sem.at[which, c]
        )

    def message(step, c):
        return pltpu.make_async_remote_copy(
            src_ref=send_s.at[step, c],
            dst_ref=recv_s.at[step, c],
            send_sem=send_sem.at[step, c],
            recv_sem=recv_sem.at[step, c],
            device_id=partners[step],
            device_id_type=MESH,
        )

    def column(k, c):
        span = pl.ds(0, HC * D)
        return pltpu.make_async_remote_copy(
            src_ref=send_s.at[UNIFORM, c],
            dst_ref=pair_s.at[c, span] if k == 0 else side_s.at[k - 1, c],
            send_sem=send_sem.at[UNIFORM + k, c],
            recv_sem=recv_sem.at[UNIFORM + k, c],
            device_id=partners[UNIFORM + k],
            device_id_type=MESH,
        )

    def forward(c):
        return pltpu.make_async_remote_copy(
            src_ref=pair_s.at[c],
            dst_ref=pair_s.at[c],
            send_sem=send_sem.at[UNIFORM + 3, c],
            recv_sem=recv_sem.at[UNIFORM + 3, c],
            device_id=partners[UNIFORM - 1],
            device_id_type=MESH,
        )

    gate_load = pltpu.make_async_copy(g_hbm, g_s, gate_sem)
    gate_load.start()

    @pl.loop(0, chunks)
    def _(c):
        load(0, c).start()
        load(1, c).start()

    @pl.loop(0, chunks)
    def _(c):
        load(2, c).start()

    pair_s[...] = jnp.zeros_like(pair_s)
    barrier = pltpu.get_barrier_semaphore()
    for partner in partners:
        pl.semaphore_signal(barrier, inc=1, device_id=partner, device_id_type=MESH)

    pl.semaphore_wait(barrier, len(partners))

    def states(c):
        load(0, c).wait()
        load(1, c).wait()
        for part in range(HC):
            h = c * HC + part
            cols = pl.ds(pl.multiple_of(h * D, D), D)
            vt = v_s[:, cols].T
            sums = [
                dot_nn(vt[:, i * TILE:(i + 1) * TILE], k_s[i * TILE:(i + 1) * TILE, cols])
                for i in range(tiles)
            ]
            first = sums[0] + sums[1]
            near_s[h, 0] = sums[0].astype(BF16)
            near_s[h, 1] = sums[2].astype(BF16)
            near_s[h, 2] = first.astype(BF16)
            total = first + (sums[2] + sums[3])
            cur_s[h] = total
            send_s[0, c, part * D:(part + 1) * D] = total.astype(BF16)
        message(0, c).start()

    def advance(step, c):
        for part in range(HC):
            h = c * HC + part
            rows_of = slice(part * D, (part + 1) * D)
            total = cur_s[h] + recv_s[step, c, rows_of].astype(F32)
            cur_s[h] = total
            send_s[step + 1, c, rows_of] = total.astype(BF16)

    def exchange(step, c):
        owner = core == c % 2
        if step < UNIFORM:
            message(step, c).wait_recv()
        if step + 1 < UNIFORM:
            advance(step, c)
            message(step + 1, c).start()
        elif step + 1 == UNIFORM:

            @pl.when(owner)
            def _():
                advance(step, c)
                for k in range(3):
                    pl.when(sends[k])(column(k, c).start)

        elif step == UNIFORM:

            @pl.when(owner)
            def _():
                pl.when(y % 2 == 1)(column(0, c).wait_recv)

                @pl.when(y >= 2)
                def _():
                    column(1, c).wait_recv()
                    column(2, c).wait_recv()
                    pair_s[c, HC * D:] = (
                        side_s[0, c].astype(F32) + side_s[1, c].astype(F32)
                    ).astype(BF16)

                forward(c).start()

        else:

            @pl.when(core != c % 2)
            def _():
                forward(c).wait_recv()

    def exchanges(slot):
        for step in reversed(range(STEPS)):
            c = slot - OFF[step]

            @pl.when((c >= 0) & (c < chunks))
            def _():
                exchange(step, c)

    def gates():
        gate_load.wait()
        row = lax.broadcasted_iota(jnp.int32, (heads * 16, heads * LEVELS), 0)
        col = lax.broadcasted_iota(jnp.int32, (heads * 16, heads * LEVELS), 1)
        pick = (col == (row // 16) * LEVELS + row % 16) & (row % 16 < LEVELS)
        table = dot_nn(jnp.where(pick, 1.0, 0.0).astype(BF16), g_s[...])
        level = lax.broadcasted_iota(jnp.int32, (heads * 16, 1), 0) % 16
        scale = jnp.zeros((heads * 16, 1), F32)
        for l in range(LEVELS):
            factor = jnp.float32((BLOCK * 2 ** max(l - 1, 0)) ** -0.5)
            if l >= FIRST_REMOTE:
                factor = factor * bits[l - FIRST_REMOTE].astype(F32)
            scale = jnp.where(level == l, factor, scale)
        gate_s[...] = (table * scale).reshape(heads, 16, rows)

    half = TILE // 2
    s_at = lax.broadcasted_iota(jnp.int32, (half, half), 0)
    t_at = lax.broadcasted_iota(jnp.int32, (half, half), 1)
    own = (s_at // BLOCK == t_at // BLOCK) & (s_at <= t_at)
    before = s_at // BLOCK < t_at // BLOCK

    def local(h):
        cols = pl.ds(pl.multiple_of(h * D, D), D)
        for i in range(tiles):
            span = slice(i * TILE, (i + 1) * TILE)
            q_tile = q_s[span, cols]
            scores = dot_nt(k_s[span, cols], q_tile)
            gate = [gate_s[h, l:l + 1, span] for l in range(3)]

            def weigh(at):
                part = slice(at, at + half)
                return jnp.where(own, gate[0][:, part], jnp.where(before, gate[1][:, part], 0.0))

            top = jnp.concatenate(
                [scores[:half, :half] * weigh(0), scores[:half, half:] * gate[2][:, half:]], axis=1
            )
            low = jnp.concatenate(
                [jnp.zeros((half, half), F32), scores[half:, half:] * weigh(half)], axis=1
            )
            weights = jnp.concatenate([top.astype(BF16), low.astype(BF16)], axis=0)
            acc_s[h, span] = dot_nn(weights.T, v_s[span, cols])

    def remote(c, part):
        h = c * HC + part
        cols = pl.ds(pl.multiple_of(h * D, D), D)
        for i in range(tiles):
            span = slice(i * TILE, (i + 1) * TILE)
            q_tile = q_s[span, cols]
            parts = [(FIRST_REMOTE + st, recv_s[st, c, part * D:(part + 1) * D]) for st in range(UNIFORM)]
            for st in range(UNIFORM, STEPS):
                at = (st - UNIFORM) * HC * D + part * D
                parts.append((FIRST_REMOTE + st, pair_s[c, at:at + D]))
            if i % 2 == 1:
                parts.append((3, near_s[h, i // 2]))
            if i >= 2:
                parts.append((4, near_s[h, 2]))
            reads = dot_nt(jnp.concatenate([state for _, state in parts], axis=0), q_tile)
            total = jnp.zeros((D, TILE), F32)
            for at, (l, _) in enumerate(parts):
                total = total + reads[at * D:(at + 1) * D] * gate_s[h, l:l + 1, span]
            o_ref[span, cols] = (total.T + acc_s[h, span]).astype(BF16)

    @pl.loop(0, chunks)
    def _(c):
        states(c)
        exchanges(c)

        @pl.when(c == GS)
        def _():
            gates()

    @pl.loop(0, chunks)
    def _(c):
        load(2, c).wait()

    @pl.loop(0, heads // LP)
    def _(n):
        exchanges(chunks + n)
        for part in range(LP):
            local(n * LP + part)

    done = chunks + heads // LP
    idle = max(0, OFF[-1] - done)

    @pl.loop(0, idle)
    def _(n):
        exchanges(done + n)

    @pl.loop(0, chunks)
    def _(c):
        exchanges(done + idle + c)
        for part in range(HC):
            remote(c, part)

    @pl.loop(0, chunks)
    def _(c):
        for step in range(UNIFORM):
            message(step, c).wait_send()

        @pl.when(core == c % 2)
        def _():
            for k in range(3):
                pl.when(sends[k])(column(k, c).wait_send)
            forward(c).wait_send()


def shards(queries, key_vectors, value_vectors, level_gates):
    rows, width = queries.shape
    heads = width // D
    chunks = heads // HC
    hbm = pl.BlockSpec(memory_space=pltpu.HBM)
    return pl.pallas_call(
        functools.partial(kernel, heads),
        out_shape=pltpu.VMEM((rows, width), BF16),
        in_specs=[hbm] * 4,
        out_specs=pl.BlockSpec(memory_space=pltpu.VMEM),
        scratch_shapes=[
            pltpu.VMEM((rows, width), BF16),
            pltpu.VMEM((rows, width), BF16),
            pltpu.VMEM((rows, width), BF16),
            pltpu.VMEM((heads * LEVELS, rows), BF16),
            pltpu.VMEM((heads, 16, rows), F32),
            pltpu.VMEM((heads, rows, D), F32),
            pltpu.VMEM((heads, D, D), F32),
            pltpu.VMEM((heads, 3, D, D), BF16),
            pltpu.VMEM((UNIFORM + 1, chunks, HC * D, D), BF16),
            pltpu.VMEM((UNIFORM, chunks, HC * D, D), BF16),
            pltpu.VMEM((chunks, 2 * HC * D, D), BF16),
            pltpu.VMEM((2, chunks, HC * D, D), BF16),
            pltpu.SemaphoreType.DMA((3, chunks)),
            pltpu.SemaphoreType.DMA,
            pltpu.SemaphoreType.DMA((UNIFORM + 4, chunks)),
            pltpu.SemaphoreType.DMA((UNIFORM + 4, chunks)),
        ],
        compiler_params=pltpu.CompilerParams(
            collective_id=0, has_side_effects=True, vmem_limit_bytes=VL * 1024 * 1024
        ),
        name="fenwick",
    )(queries, key_vectors, value_vectors, level_gates.T)


def solution(mesh):
    spec = P(("ctx", "uly"), None)
    return jax.shard_map(
        shards, mesh=mesh, in_specs=(spec,) * 4, out_specs=spec, check_vma=False
    )
```
